256 devices in a mesh: blk: 64 (over y, z_hi, x, core), frm: 4 (over z_lo).
Axes of the slice: x: 4, y: 4, z: 8 (z_hi: 2, z_lo: 4; z = z_hi * 4 + z_lo), core: 2. Of those that a mesh axis runs over, the one named last changes fastest.
Arguments:
- activity: float32 [100352, 1536], P('blk', 'frm')
- plan: int32 [2], replicated, may hold values from 1 to 63, as said below
Outputs:
- connectivity: bfloat16 [2, 100352, 1568], P(None, ('blk', 'frm'))
The draws below stay inside these ranges and needn't reach their ends.
Inputs may be any that keep to these rules, and one draw needn't show every extreme that they name: `plan`: some round's offset equals 63.
All inputs are finite; a program needn't handle non-finite values.
Results may differ from the reference program's by a relative error of at most 0.0058.
Values may be sent and summed in bfloat16 or wider, within the bound.
A program may use at most 128 MiB of HBM per device.

```python
import math
import jax
import jax.numpy as jnp
from jax import lax

BLOCK = 1568
T_DEV = 384
ROUNDS = 2
NEURONS = 100352
FRAMES = 1536
N_BLK = 64
N_FRM = 4


def draw_activity(key, part):
    key = jax.random.fold_in(key, 5)
    keys = jax.random.split(key, 3)
    scales = jnp.exp(jax.random.uniform(keys[0], (NEURONS, N_FRM, 1), jnp.float32, math.log(0.5), math.log(8.0)))
    baseline = jax.random.uniform(keys[1], (NEURONS, N_FRM, 1), jnp.float32, -2.0, 2.0)
    noise = jax.random.normal(keys[2], (NEURONS, N_FRM, T_DEV), jnp.float32)
    return (baseline + scales * noise).reshape(NEURONS, FRAMES).astype(jnp.float32)


def draw_plan(key, part):
    key = jax.random.fold_in(key, 11)
    keys = jax.random.split(key, 2)
    others = jax.random.randint(keys[0], (ROUNDS,), 1, N_BLK - 1)
    farthest = jax.random.randint(keys[1], (), 0, ROUNDS)
    slots = jnp.arange(ROUNDS)
    return jnp.where(slots == farthest, N_BLK - 1, others).astype(jnp.int32)


def setup_inputs(seed: int = 0) -> dict:
    key_of = jax.random.split(jax.random.key(seed), 3)
    activity = draw_activity(jax.random.fold_in(key_of[2], 71), 0)
    plan = draw_plan(jax.random.fold_in(key_of[2], 71), 0)
    return dict(activity=activity, plan=plan)


EPS = 1e-05

def standardize(activity):
    sliced = activity.reshape(NEURONS, N_FRM, T_DEV)
    mean = lax.optimization_barrier(jnp.mean(sliced, axis=2, keepdims=True))
    centred = sliced - mean
    spread = lax.optimization_barrier(jnp.mean(centred * centred, axis=2, keepdims=True))
    return (centred * lax.rsqrt(spread + EPS)).reshape(NEURONS, FRAMES).astype(jnp.bfloat16)

def reference(activity, plan):
    scores = standardize(activity).reshape(N_BLK, BLOCK, FRAMES)
    factor = 1.0 / math.sqrt(FRAMES)
    indices = jnp.arange(N_BLK, dtype=jnp.int32)
    results = []
    for turn in range(ROUNDS):
        key_now = plan[turn].astype(jnp.int32)

        def one_block(index):
            home = scores[index].astype(jnp.float32)
            other = scores[jnp.remainder(index + key_now, N_BLK).astype(jnp.int32)].astype(jnp.float32)
            total = lax.dot_general(home, other, (((1,), (1,)), ((), ())), precision=lax.Precision.HIGHEST, preferred_element_type=jnp.float32)
            return total * factor
        results.append(lax.map(one_block, indices).reshape(NEURONS, BLOCK))
    return jnp.stack(results).astype(jnp.bfloat16)
```

```python
from functools import partial
import math

import jax
import jax.numpy as jnp
from jax import lax
from jax.experimental import pallas as pl
from jax.experimental.pallas import tpu as pltpu
from jax.sharding import PartitionSpec as P

EPS = 1e-05
MESH = pl.DeviceIdType.MESH
AXES = ("blk", "frm")
PARTS = 4
STEP = 512


def standardize(activity):
    mean = jnp.mean(activity, axis=1, keepdims=True)
    centred = activity - mean
    spread = jnp.mean(centred * centred, axis=1, keepdims=True)
    return (centred * lax.rsqrt(spread + EPS)).astype(jnp.bfloat16)


def pull(scores, distance):
    blocks = lax.axis_size("blk")

    def pairs(sources, targets):
        return [
            (((b + distance) % blocks) * PARTS + s, b * PARTS + t)
            for b in range(blocks)
            for s, t in zip(sources, targets)
        ]

    own = lax.ppermute(scores, AXES, pairs((1, 2), (1, 2)))
    end = lax.ppermute(scores, AXES, pairs((0, 3), (1, 2)))
    return own, end


def column_chunks(size):
    starts = list(range(0, size - STEP + 1, STEP)) if size >= STEP else [0]
    return [(a, (starts[i + 1] if i + 1 < len(starts) else size) - a) for i, a in enumerate(starts)]


def kernel(factor, parts_ref, scores_ref, own_ref, end_ref, out_ref, left, right, tx, rx, fin,
           local_sem, h_send, h_recv, end_send, end_recv, own_send, own_recv, mid_send, mid_recv,
           out_send, out_recv, keep_sem):
    size, frames = scores_ref.shape
    blocks = lax.axis_size("blk")
    chunks = column_chunks(size)
    b, f = lax.axis_index("blk"), lax.axis_index("frm")
    after, before = lax.rem(b + 1, blocks), lax.rem(b + blocks - 1, blocks)
    half = f // 2
    centre, end = 1 + half, 3 * half
    far = [(1 - half) * (3 - i) + half * i for i in range(2)]
    near = [half * (3 - i) + (1 - half) * i for i in range(2)]
    order = far + near
    is_centre = f == centre
    lane_own, lane_end = pl.ds(0, frames), pl.ds(frames, frames)

    def send_part(i):
        return pltpu.make_async_remote_copy(
            src_ref=parts_ref.at[order[i]], dst_ref=left.at[order[i], :, lane_end],
            send_sem=h_send.at[i], recv_sem=h_recv.at[i],
            device_id=(b, centre), device_id_type=MESH)

    def send_end(q):
        rows = pl.ds(*chunks[q])
        return pltpu.make_async_remote_copy(
            src_ref=scores_ref.at[rows], dst_ref=right.at[1, rows, lane_end],
            send_sem=end_send.at[q], recv_sem=end_recv.at[q],
            device_id=(after, centre), device_id_type=MESH)

    def send_own(q):
        rows = pl.ds(*chunks[q])
        return pltpu.make_async_remote_copy(
            src_ref=scores_ref.at[rows], dst_ref=right.at[1, rows, lane_own],
            send_sem=own_send.at[q], recv_sem=own_recv.at[q],
            device_id=(after, centre), device_id_type=MESH)

    def send_mid(r, i, q):
        start = chunks[q][0]
        stop = chunks[q + 1][0] if q + 1 < len(chunks) else tx.shape[-1]
        lanes = pl.ds(start, stop - start)
        return pltpu.make_async_remote_copy(
            src_ref=tx.at[r, i, :, lanes], dst_ref=rx.at[r, i, :, lanes],
            send_sem=mid_send.at[r, i, q], recv_sem=mid_recv.at[r, i, q],
            device_id=(b, 3 - centre), device_id_type=MESH)

    def send_out(r):
        return pltpu.make_async_remote_copy(
            src_ref=fin.at[r, 0], dst_ref=out_ref.at[r],
            send_sem=out_send.at[r], recv_sem=out_recv.at[r],
            device_id=(b, end), device_id_type=MESH)

    def keep_out(r):
        return pltpu.make_async_copy(fin.at[r, 1], out_ref.at[r], keep_sem.at[r])

    def product(r, part, q):
        rows = pl.ds(*chunks[q])
        return lax.dot_general(left[part], right[r, rows, :], (((1,), (1,)), ((), ())),
                               preferred_element_type=jnp.float32)

    barrier = pltpu.get_barrier_semaphore()

    def greet(*device):
        pl.semaphore_signal(barrier, inc=1, device_id=device, device_id_type=MESH)

    @pl.when(jnp.logical_not(is_centre))
    def _():
        greet(b, centre)
        pl.semaphore_wait(barrier, 2)
        for i in range(2):
            send_part(i).start()
        for q in range(len(chunks)):
            send_end(q).start()
        for i in range(2, 4):
            send_part(i).start()
        for i in range(4):
            send_part(i).wait_send()
        for q in range(len(chunks)):
            send_end(q).wait_send()
        for r in range(2):
            send_out(r).wait_recv()

    @pl.when(is_centre)
    def _():
        greet(b, end)
        greet(before, end)
        greet(before, f)
        greet(b, 3 - f)
        locals_ = [
            pltpu.make_async_copy(parts_ref, left.at[:, :, lane_own], local_sem.at[0]),
            pltpu.make_async_copy(own_ref, right.at[0, :, lane_own], local_sem.at[1]),
            pltpu.make_async_copy(end_ref, right.at[0, :, lane_end], local_sem.at[2]),
        ]
        for copy in locals_:
            copy.start()
        pl.semaphore_wait(barrier, 3)
        for q in range(len(chunks)):
            send_own(q).start()
        for copy in locals_:
            copy.wait()
        for r in range(2):
            for i in range(2):
                if r == 0:
                    send_part(i).wait_recv()
                for q in range(len(chunks)):
                    if r == 1 and i == 0:
                        send_own(q).wait_recv()
                        send_end(q).wait_recv()
                    start, width = chunks[q]
                    tx[r, i, :, pl.ds(start, width)] = product(r, far[i], q).astype(tx.dtype)
                    send_mid(r, i, q).start()
        for r in range(2):
            for i in range(2):
                if r == 0:
                    send_part(2 + i).wait_recv()
                for q in range(len(chunks)):
                    start, width = chunks[q]
                    lanes = pl.ds(start, width)
                    mine = product(r, near[i], q)
                    send_mid(r, i, q).wait_recv()
                    total = mine + rx[r, i, :, lanes].astype(jnp.float32)
                    fin[r, i, :, lanes] = (total * factor).astype(fin.dtype)
                if i == 0:
                    send_out(r).start()
                else:
                    keep_out(r).start()
        for r in range(2):
            send_out(r).wait_send()
            keep_out(r).wait()
            for i in range(2):
                for q in range(len(chunks)):
                    send_mid(r, i, q).wait_send()
        for q in range(len(chunks)):
            send_own(q).wait_send()


def products(scores, own, end):
    size, frames = scores.shape
    rows = size // PARTS
    chunks = len(column_chunks(size))
    padded = -(-size // 128) * 128
    factor = 1.0 / math.sqrt(frames * PARTS)
    dma = pltpu.SemaphoreType.DMA
    return pl.pallas_call(
        partial(kernel, factor),
        name="pair_products",
        out_shape=jax.ShapeDtypeStruct((2, rows, size), jnp.bfloat16),
        in_specs=[pl.BlockSpec(memory_space=pl.ANY)] * 4,
        out_specs=pl.BlockSpec(memory_space=pl.ANY),
        scratch_shapes=[
            pltpu.VMEM((PARTS, rows, 2 * frames), jnp.bfloat16),
            pltpu.VMEM((2, size, 2 * frames), jnp.bfloat16),
            pltpu.VMEM((2, 2, rows, padded), jnp.bfloat16),
            pltpu.VMEM((2, 2, rows, padded), jnp.bfloat16),
            pltpu.VMEM((2, 2, rows, size), jnp.bfloat16),
            dma((3,)), dma((4,)), dma((4,)), dma((chunks,)), dma((chunks,)), dma((chunks,)), dma((chunks,)),
            dma((2, 2, chunks)), dma((2, 2, chunks)), dma((2,)), dma((2,)), dma((2,)),
        ],
        compiler_params=pltpu.CompilerParams(
            collective_id=0, has_side_effects=True, vmem_limit_bytes=48 * 2**20),
        cost_estimate=pl.CostEstimate(
            flops=8 * size * size * frames, bytes_accessed=20 * size * frames, transcendentals=0),
    )(scores.reshape(PARTS, rows, frames), scores, own, end)


def per_device(activity, plan):
    scores = standardize(activity)
    blocks = lax.axis_size("blk")
    first_last = plan[0] == blocks - 1
    distance = jnp.where(first_last, plan[1], plan[0])
    branches = [partial(pull, distance=d) for d in range(1, blocks)]
    own, end = lax.switch(distance - 1, branches, scores)
    both = products(scores, own, end)
    return jnp.where(first_last, both[::-1], both)


def solution(mesh):
    in_specs = (P("blk", "frm"), P())
    out_specs = P(None, ("blk", "frm"), None)
    return jax.shard_map(
        per_device, mesh=mesh, in_specs=in_specs, out_specs=out_specs, check_vma=False
    )
```

```python
from functools import partial
import math

import jax
import jax.numpy as jnp
from jax import lax
from jax.experimental import pallas as pl
from jax.experimental.pallas import tpu as pltpu
from jax.sharding import PartitionSpec as P

EPS = 1e-05
MESH = pl.DeviceIdType.MESH
PARTS = 4
CHUNKS = 7
TILE = 256
SLAB = 128
DEPTH = 512
HALF_RING = 8
AHEAD = 2


def standardize(activity):
    mean = jnp.mean(activity, axis=1, keepdims=True)
    centred = activity - mean
    spread = jnp.mean(centred * centred, axis=1, keepdims=True)
    return (centred * lax.rsqrt(spread + EPS)).astype(jnp.bfloat16)


def kernel(distance, factor, parts_ref, scores_ref, out_ref, left, right, fin, acc,
           local_sem, h_send, h_recv, pp_send, pp_recv, fwd_send, fwd_recv, out_send, out_recv, keep_sem):
    size, frames = scores_ref.shape
    blocks = lax.axis_size("blk")
    piece = size // CHUNKS
    tiles = fin.shape[-1] // TILE
    slabs = out_ref.shape[-1] // SLAB
    shifts = (blocks - 1, distance)
    b, f = lax.axis_index("blk"), lax.axis_index("frm")
    half = f // 2
    inner = f * (3 - f) // 2
    outer = 1 - inner
    centre, end, other = 1 + half, 3 * half, 2 - half

    def far(i):
        return (1 - half) * (3 - i) + half * i

    def near(i):
        return half * (3 - i) + (1 - half) * i

    def lanes(slice_index):
        return pl.ds(pl.multiple_of(slice_index * frames, 128), frames)

    def crossing(one, two):
        return lax.rem(one // HALF_RING + two // HALF_RING, 2)

    def target(shift):
        block = lax.rem(b + (blocks - shift), blocks)
        return block, 1 + lax.rem(half + crossing(b, block), 2)

    def source(shift):
        block = lax.rem(b + shift, blocks)
        return block, lax.rem(half + crossing(b, block), 2)

    targets = [target(shift) for shift in shifts]
    sources = [source(shift) for shift in shifts]

    def of_round(r, pair):
        return pair[0] * (1 - r) + pair[1] * r

    def loop(stop, act, start=0):
        def body(i, carry):
            act(i)
            return carry
        lax.fori_loop(start, stop, body, 0)

    def remote(src, dst, send, recv, device):
        return pltpu.make_async_remote_copy(
            src_ref=src, dst_ref=dst, send_sem=send, recv_sem=recv, device_id=device, device_id_type=MESH)

    def part_in(i):
        return remote(parts_ref.at[near(i)], left.at[i, :, lanes(f)], h_send.at[0, i], h_recv.at[0, i], (b, centre))

    def part_across(i):
        return remote(parts_ref.at[far(i)], left.at[i, :, lanes(f)], h_send.at[1, i], h_recv.at[1 + outer, i], (b, other))

    def part_arrives(i, kind):
        return remote(parts_ref.at[i], left.at[i, :, lanes(f)], h_send.at[0, i], h_recv.at[kind, i], (b, other))

    def part_own(i):
        return pltpu.make_async_copy(parts_ref.at[near(i)], left.at[i, :, lanes(f)], local_sem.at[i])

    def rows_of(q):
        return pl.ds(pl.multiple_of(q * piece, 16), piece)

    def slice_out(r, q):
        rows = rows_of(q)
        device = tuple(of_round(r, pair) for pair in zip(*targets))
        return remote(scores_ref.at[rows], right.at[r, rows, lanes(f)], pp_send.at[r, q], pp_recv.at[r, q, outer], device)

    def slice_arrives(r, q, kind):
        rows = rows_of(q)
        return remote(scores_ref.at[rows], right.at[r, rows, lanes(f)], pp_send.at[r, q], pp_recv.at[r, q, kind], (b, other))

    def pass_on(r, q, kind):
        h = of_round(r, [side for _, side in sources])
        where = right.at[r, rows_of(q), lanes((1 + h) * (1 - kind) + 3 * h * kind)]
        return remote(where, where, fwd_send.at[r, q, kind], fwd_recv.at[r, q, kind], (b, other))

    def columns(j):
        return pl.ds(pl.multiple_of(j * SLAB, SLAB), SLAB)

    def result_out(r, j):
        return remote(fin.at[r, 0, :, columns(j)], out_ref.at[r, :, columns(j)], out_send.at[r, j], out_recv.at[r, j], (b, end))

    def result_kept(r, j):
        return pltpu.make_async_copy(fin.at[r, 1, :, columns(j)], out_ref.at[r, :, columns(j)], keep_sem.at[r, j])

    barrier = pltpu.get_barrier_semaphore()

    def greet(block, frm):
        pl.semaphore_signal(barrier, inc=1, device_id=(block, frm), device_id_type=MESH)

    @pl.when(inner == 0)
    def _():
        greet(b, centre)

    @pl.when(inner == 1)
    def _():
        loop(2, lambda i: part_own(i).start())
        greet(b, end)
        greet(b, 3 - end)
        greet(b, other)
        for block, side in sources:
            greet(block, 1 + side)
            greet(block, 3 * side)
    pl.semaphore_wait(barrier, 4)

    loop(2, lambda i: part_across(i).start())

    @pl.when(inner == 0)
    def _():
        loop(2, lambda i: part_in(i).start())

    def send_slices(t):
        r, q = t // CHUNKS, lax.rem(t, CHUNKS)

        @pl.when(outer * r == 1)
        def _():
            slice_out(0, q).wait_send()
        slice_out(r, q).start()
    loop(2 * CHUNKS, send_slices)

    def work(r, j):
        cols = pl.ds(pl.multiple_of(j * TILE, TILE), TILE)

        def half_rows(i):
            def add(k):
                deep = pl.ds(pl.multiple_of(k * DEPTH, 128), DEPTH)
                acc[...] += lax.dot_general(
                    left[i, :, deep], right[r, cols, deep], (((1,), (1,)), ((), ())),
                    preferred_element_type=jnp.float32)
            acc[...] = jnp.zeros_like(acc)
            loop(PARTS * frames // DEPTH, add)
            fin[r, i, :, cols] = (acc[...] * factor).astype(fin.dtype)
        loop(2, half_rows)

        def hand_in(slab):
            result_out(r, slab).start()
            result_kept(r, slab).start()
        loop(jnp.minimum((j + 1) * (TILE // SLAB), slabs), hand_in, j * (TILE // SLAB))

    @pl.when(inner == 1)
    def _():
        def step(t):
            @pl.when(t < 2 * CHUNKS)
            def _():
                def forward(kind):
                    r, q = t // CHUNKS, lax.rem(t, CHUNKS)
                    slice_arrives(r, q, kind).wait_recv()
                    pass_on(r, q, kind).start()
                loop(2, forward)

            @pl.when(t == AHEAD)
            def _():
                def rows_there(i):
                    part_own(i).wait()
                    loop(3, lambda kind: part_arrives(i, kind).wait_recv())
                loop(2, rows_there)

            @pl.when(t >= AHEAD)
            def _():
                r, q = (t - AHEAD) // CHUNKS, lax.rem(t - AHEAD, CHUNKS)
                loop(2, lambda kind: pass_on(r, q, kind).wait_recv())
                stop = jnp.where(q == CHUNKS - 1, tiles, (q + 1) * piece // TILE)
                loop(stop, lambda j: work(r, j), q * piece // TILE)
        loop(2 * CHUNKS + AHEAD, step)

        def drain(t):
            r, q = t // CHUNKS, lax.rem(t, CHUNKS)
            slice_out(r, q).wait_send()
            loop(2, lambda kind: pass_on(r, q, kind).wait_send())
        loop(2 * CHUNKS, drain)

        def drain_results(t):
            r, j = t // slabs, lax.rem(t, slabs)
            result_out(r, j).wait_send()
            result_kept(r, j).wait()
        loop(2 * slabs, drain_results)

    loop(2, lambda i: part_across(i).wait_send())

    @pl.when(inner == 0)
    def _():
        loop(2, lambda i: part_in(i).wait_send())
        loop(CHUNKS, lambda q: slice_out(1, q).wait_send())
        loop(2 * slabs, lambda t: result_out(t // slabs, lax.rem(t, slabs)).wait_recv())


def products(parts, scores, distance):
    size, frames = scores.shape
    rows = size // PARTS
    tiles, slabs = -(-size // TILE), -(-size // SLAB)
    factor = 1.0 / math.sqrt(frames * PARTS)
    dma = pltpu.SemaphoreType.DMA
    return pl.pallas_call(
        partial(kernel, distance, factor),
        name="pair_products",
        out_shape=jax.ShapeDtypeStruct((2, rows, slabs * SLAB), jnp.bfloat16),
        in_specs=[pl.BlockSpec(memory_space=pl.ANY)] * 2,
        out_specs=pl.BlockSpec(memory_space=pl.ANY),
        scratch_shapes=[
            pltpu.VMEM((2, rows, PARTS * frames), jnp.bfloat16),
            pltpu.VMEM((2, tiles * TILE, PARTS * frames), jnp.bfloat16),
            pltpu.VMEM((2, 2, rows, tiles * TILE), jnp.bfloat16),
            pltpu.VMEM((rows, TILE), jnp.float32),
            dma((2,)), dma((2, 2)), dma((3, 2)),
            dma((2, CHUNKS)), dma((2, CHUNKS, 2)), dma((2, CHUNKS, 2)), dma((2, CHUNKS, 2)),
            dma((2, slabs)), dma((2, slabs)), dma((2, slabs)),
        ],
        compiler_params=pltpu.CompilerParams(
            collective_id=distance, has_side_effects=True, vmem_limit_bytes=40 * 2**20),
        cost_estimate=pl.CostEstimate(
            flops=8 * size * size * frames, bytes_accessed=20 * size * frames, transcendentals=0),
    )(parts, scores)


def per_device(activity, plan):
    scores = standardize(activity)
    size, frames = scores.shape
    parts = scores.reshape(PARTS, size // PARTS, frames)
    blocks = lax.axis_size("blk")
    first_last = plan[0] == blocks - 1
    distance = jnp.where(first_last, plan[1], plan[0])
    branches = [partial(products, distance=d) for d in range(1, blocks)]
    both = lax.switch(distance - 1, branches, parts, scores)
    return jnp.where(first_last, both, both[::-1])[:, :, :size]


def solution(mesh):
    in_specs = (P("blk", "frm"), P())
    out_specs = P(None, ("blk", "frm"), None)
    return jax.shard_map(
        per_device, mesh=mesh, in_specs=in_specs, out_specs=out_specs, check_vma=False
    )
```

```python
from functools import partial
import math

import jax
import jax.numpy as jnp
from jax import lax
from jax.experimental import pallas as pl
from jax.experimental.pallas import tpu as pltpu
from jax.sharding import PartitionSpec as P

EPS = 1e-05
MESH = pl.DeviceIdType.MESH
PARTS = 4
CHUNKS = 7
TILE = 256
ROW = 8
DEPTH = 512
AHEAD = 4
FLIGHT = 2


def standardize(activity):
    mean = jnp.mean(activity, axis=1, keepdims=True)
    centred = activity - mean
    spread = jnp.mean(centred * centred, axis=1, keepdims=True)
    return (centred * lax.rsqrt(spread + EPS)).astype(jnp.bfloat16)


def loop(stop, act, start=0):
    def body(i, carry):
        act(i)
        return carry
    lax.fori_loop(start, stop, body, 0)


def remote(src, dst, send, recv, device):
    return pltpu.make_async_remote_copy(
        src_ref=src, dst_ref=dst, send_sem=send, recv_sem=recv, device_id=device, device_id_type=MESH)


class Place:
    def __init__(self):
        self.blocks = lax.axis_size("blk")
        self.b, self.f = lax.axis_index("blk"), lax.axis_index("frm")
        self.half = self.f // 2
        self.inner = self.f * (3 - self.f) // 2
        self.outer = 1 - self.inner
        self.centre, self.end, self.other = 1 + self.half, 3 * self.half, 2 - self.half

    def crossing(self, one, two):
        return lax.rem(one // ROW + two // ROW, 2)

    def target(self, shift):
        block = lax.rem(self.b + (self.blocks - shift), self.blocks)
        return block, 1 + lax.rem(self.half + self.crossing(self.b, block), 2)

    def source(self, shift):
        block = lax.rem(self.b + shift, self.blocks)
        return block, lax.rem(self.half + self.crossing(self.b, block), 2)

    def far(self, i):
        return (1 - self.half) * (3 - i) + self.half * i

    def near(self, i):
        return self.half * (3 - i) + (1 - self.half) * i


def greet(block, frm):
    pl.semaphore_signal(pltpu.get_barrier_semaphore(), inc=1, device_id=(block, frm), device_id_type=MESH)


def gather_kernel(high, parts_ref, scores_ref, left, right, moved,
                  own_sem, h_send, h_recv, pp_send, pp_recv, fwd_send, fwd_recv, move_send, move_recv):
    size, frames = scores_ref.shape
    piece = size // CHUNKS
    at = Place()
    mirrored = high % 2
    shift = at.blocks - 1

    def lanes(frame_slice):
        slot = 3 - frame_slice if mirrored else frame_slice
        return pl.ds(pl.multiple_of(slot * frames, 128), frames)

    def part_in(i):
        return remote(parts_ref.at[at.near(i)], left.at[i, :, lanes(at.f)], h_send.at[0, i], h_recv.at[0, i],
                      (at.b, at.centre))

    def part_across(i):
        return remote(parts_ref.at[at.far(i)], left.at[i, :, lanes(at.f)], h_send.at[1, i],
                      h_recv.at[1 + at.outer, i], (at.b, at.other))

    def part_arrives(i, kind):
        return remote(parts_ref.at[i], left.at[i, :, lanes(at.f)], h_send.at[0, i], h_recv.at[kind, i],
                      (at.b, at.other))

    def part_own(i):
        return pltpu.make_async_copy(parts_ref.at[at.near(i)], left.at[i, :, lanes(at.f)], own_sem.at[i])

    def rows_of(q):
        return pl.ds(pl.multiple_of(q * piece, 16), piece)

    aim = at.target(shift)
    _, side = at.source(shift)

    def slice_out(q):
        rows = rows_of(q)
        return remote(scores_ref.at[rows], right.at[rows, lanes(at.f)], pp_send.at[q], pp_recv.at[q, at.outer], aim)

    def slice_arrives(q, kind):
        rows = rows_of(q)
        return remote(scores_ref.at[rows], right.at[rows, lanes(at.f)], pp_send.at[q], pp_recv.at[q, kind],
                      (at.b, at.other))

    def pass_on(q, kind):
        where = right.at[rows_of(q), lanes((1 + side) * (1 - kind) + 3 * side * kind)]
        return remote(where, where, fwd_send.at[q, kind], fwd_recv.at[q, kind], (at.b, at.other))

    place = 3 - at.f if mirrored else at.f
    if high:
        move = remote(scores_ref, moved, move_send.at[0], move_recv.at[0],
                      (lax.rem(at.b + (at.blocks - ROW * high), at.blocks), place))
        greet(lax.rem(at.b + ROW * high, at.blocks), place)
    else:
        move = pltpu.make_async_copy(scores_ref, moved, move_send.at[0])

    @pl.when(at.inner == 0)
    def _():
        greet(at.b, at.centre)

    @pl.when(at.inner == 1)
    def _():
        loop(2, lambda i: part_own(i).start())
        greet(at.b, at.end)
        greet(at.b, 3 - at.end)
        greet(at.b, at.other)
        block, side = at.source(shift)
        greet(block, 1 + side)
        greet(block, 3 * side)

    pl.semaphore_wait(pltpu.get_barrier_semaphore(), 3 + (1 if high else 0))

    loop(2, lambda i: part_across(i).start())
    loop(FLIGHT, lambda q: slice_out(q).start())
    if not mirrored:
        move.start()

    def next_slice(q):
        slice_out(q).wait_send()

        @pl.when(q + FLIGHT < CHUNKS)
        def _():
            slice_out(q + FLIGHT).start()

    @pl.when(at.inner == 0)
    def _():
        loop(CHUNKS, next_slice)
        loop(2, lambda i: part_in(i).start())
        if mirrored:
            move.start()
        loop(2, lambda i: part_in(i).wait_send())

    @pl.when(at.inner == 1)
    def _():
        def forward(q):
            next_slice(q)

            def one(kind):
                slice_arrives(q, kind).wait_recv()
                pass_on(q, kind).start()
            loop(2, one)
            if mirrored:
                @pl.when(q == CHUNKS // 2)
                def _():
                    move.start()
        loop(CHUNKS, forward)

        def rows_there(i):
            part_own(i).wait()
            loop(3, lambda kind: part_arrives(i, kind).wait_recv())
        loop(2, rows_there)
        loop(CHUNKS, lambda q: loop(2, lambda kind: pass_on(q, kind).wait_recv()))
        loop(CHUNKS, lambda q: loop(2, lambda kind: pass_on(q, kind).wait_send()))

    loop(2, lambda i: part_across(i).wait_send())
    move.wait()


def product_kernel(low, factor, left_ref, right_ref, moved, out_ref, left, right, fin, acc,
                   own_sem, pp_send, pp_recv, fwd_send, fwd_recv, out_send, out_recv, keep_sem):
    size, frames = moved.shape
    piece = size // CHUNKS
    tiles = -(-size // TILE)
    at = Place()

    def lanes(slot):
        return pl.ds(pl.multiple_of(slot * frames, 128), frames)

    def rows_of(q):
        return pl.ds(pl.multiple_of(q * piece, 16), piece)

    block, centre = at.target(low)
    aim = (block, centre * at.inner + 3 * (centre - 1) * at.outer) if low else (at.b, at.centre)
    origin, side = at.source(low)

    def slice_out(q):
        rows = rows_of(q)
        return remote(moved.at[rows], right.at[1, rows, lanes(at.f)], pp_send.at[q], pp_recv.at[q, at.outer], aim)

    def slice_arrives(q, kind):
        rows = rows_of(q)
        return remote(moved.at[rows], right.at[1, rows, lanes(at.f)], pp_send.at[q], pp_recv.at[q, kind],
                      (at.b, at.other))

    def next_slice(q):
        slice_out(q).wait_send()

        @pl.when(q + FLIGHT < CHUNKS)
        def _():
            slice_out(q + FLIGHT).start()

    def hand_over(q):
        where = right.at[1, rows_of(q), lanes(3 * side)]
        return remote(where, where, fwd_send.at[q, 1], pp_recv.at[q, 1], (at.b, at.centre))

    def slice_own(q):
        rows = rows_of(q)
        return pltpu.make_async_copy(moved.at[rows], right.at[1, rows, lanes(at.f)], pp_send.at[q])

    def pass_on(q, kind):
        where = right.at[1, rows_of(q), lanes((1 + side) * (1 - kind) + 3 * side * kind)]
        return remote(where, where, fwd_send.at[q, kind], fwd_recv.at[q, kind], (at.b, at.other))

    def tile(j, act):
        @pl.when(j < tiles - 1)
        def _():
            act(pl.ds(pl.multiple_of(j * TILE, TILE), TILE))

        @pl.when(j == tiles - 1)
        def _():
            act(pl.ds((tiles - 1) * TILE, size - (tiles - 1) * TILE))

    def result_out(r, j, cols):
        return remote(fin.at[r, 0, :, cols], out_ref.at[r, :, cols], out_send.at[r, j], out_recv.at[r, j],
                      (at.b, at.end))

    def result_kept(r, j, cols):
        return pltpu.make_async_copy(fin.at[r, 1, :, cols], out_ref.at[r, :, cols], keep_sem.at[r, j])

    def work(r, j):
        def columns(cols):
            def half_rows(i):
                def add(k):
                    deep = pl.ds(pl.multiple_of(k * DEPTH, 128), DEPTH)
                    acc[:, :cols.size] += lax.dot_general(
                        left[i, :, deep], right[r, cols, deep], (((1,), (1,)), ((), ())),
                        preferred_element_type=jnp.float32)
                acc[...] = jnp.zeros_like(acc)
                loop(PARTS * frames // DEPTH, add)
                fin[r, i, :, cols] = (acc[:, :cols.size] * factor).astype(fin.dtype)
            loop(2, half_rows)
            result_out(r, j, cols).start()
            result_kept(r, j, cols).start()
        tile(j, columns)

    loads = [
        pltpu.make_async_copy(left_ref, left, own_sem.at[0]),
        pltpu.make_async_copy(right_ref, right.at[0], own_sem.at[1]),
    ]
    barrier = pltpu.get_barrier_semaphore()

    @pl.when(at.inner == 0)
    def _():
        greet(at.b, at.centre)
        if low:
            greet(origin, 3 * side)
        pl.semaphore_wait(barrier, 2 if low else 1)
        loop(FLIGHT, lambda q: slice_out(q).start())
        if low:
            def relay(q):
                next_slice(q)
                slice_arrives(q, 1).wait_recv()
                hand_over(q).start()
            loop(CHUNKS, relay)
            loop(CHUNKS, lambda q: hand_over(q).wait_send())
        else:
            loop(CHUNKS, next_slice)
        for r in range(2):
            loop(tiles, lambda j: tile(j, lambda cols: result_out(r, j, cols).wait_recv()))

    @pl.when(at.inner == 1)
    def _():
        greet(at.b, at.other)
        greet(at.b, at.end)
        if low:
            greet(origin, 1 + side)
            pl.semaphore_wait(barrier, 3)
            loop(FLIGHT, lambda q: slice_out(q).start())
        else:
            loop(CHUNKS, lambda q: slice_own(q).start())
            pl.semaphore_wait(barrier, 2)
        for load in loads:
            load.start()

        def forward(q):
            if low:
                next_slice(q)
                slice_arrives(q, 0).wait_recv()
            else:
                slice_own(q).wait()
            pass_on(q, 0).start()
            slice_arrives(q, 1).wait_recv()
            pass_on(q, 1).start()
        for load in loads:
            load.wait()

        def first_round(j):
            work(0, j)

            @pl.when(j >= tiles - AHEAD)
            def _():
                forward(j - (tiles - AHEAD))
        loop(tiles, first_round)

        def step(t):
            @pl.when(t + AHEAD < CHUNKS)
            def _():
                forward(t + AHEAD)
            loop(2, lambda kind: pass_on(t, kind).wait_recv())
            loop(jnp.where(t == CHUNKS - 1, tiles, (t + 1) * piece // TILE), lambda j: work(1, j), t * piece // TILE)
        loop(CHUNKS, step)

        def drain(q):
            loop(2, lambda kind: pass_on(q, kind).wait_send())
        loop(CHUNKS, drain)

        def drain_results(t):
            r, j = t // tiles, lax.rem(t, tiles)

            def act(cols):
                result_out(r, j, cols).wait_send()
                result_kept(r, j, cols).wait()
            tile(j, act)
        loop(2 * tiles, drain_results)


ANY = pl.BlockSpec(memory_space=pl.ANY)


def gather(parts, scores, high):
    size, frames = scores.shape
    rows = size // PARTS
    dma = pltpu.SemaphoreType.DMA
    return pl.pallas_call(
        partial(gather_kernel, high),
        name="gather_rows",
        out_shape=[
            jax.ShapeDtypeStruct((2, rows, PARTS * frames), jnp.bfloat16),
            jax.ShapeDtypeStruct((size, PARTS * frames), jnp.bfloat16),
            jax.ShapeDtypeStruct((size, frames), jnp.bfloat16),
        ],
        in_specs=[ANY] * 2,
        out_specs=[ANY] * 3,
        scratch_shapes=[
            dma((2,)), dma((2, 2)), dma((3, 2)), dma((CHUNKS,)), dma((CHUNKS, 2)), dma((CHUNKS, 2)), dma((CHUNKS, 2)),
            dma((1,)), dma((1,)),
        ],
        compiler_params=pltpu.CompilerParams(
            collective_id=high, has_side_effects=True, vmem_limit_bytes=4 * 2**20),
        cost_estimate=pl.CostEstimate(flops=0, bytes_accessed=20 * size * frames, transcendentals=0),
    )(parts, scores)


def products(left, right, moved, low):
    size, frames = moved.shape
    rows = size // PARTS
    tiles = -(-size // TILE)
    factor = 1.0 / math.sqrt(frames * PARTS)
    dma = pltpu.SemaphoreType.DMA
    return pl.pallas_call(
        partial(product_kernel, low, factor),
        name="pair_products",
        out_shape=jax.ShapeDtypeStruct((2, rows, size), jnp.bfloat16),
        in_specs=[ANY] * 3,
        out_specs=ANY,
        scratch_shapes=[
            pltpu.VMEM((2, rows, PARTS * frames), jnp.bfloat16),
            pltpu.VMEM((2, size, PARTS * frames), jnp.bfloat16),
            pltpu.VMEM((2, 2, rows, size), jnp.bfloat16),
            pltpu.VMEM((rows, TILE), jnp.float32),
            dma((2,)), dma((CHUNKS,)), dma((CHUNKS, 2)), dma((CHUNKS, 2)), dma((CHUNKS, 2)),
            dma((2, tiles)), dma((2, tiles)), dma((2, tiles)),
        ],
        compiler_params=pltpu.CompilerParams(
            collective_id=ROW + low, has_side_effects=True, vmem_limit_bytes=32 * 2**20),
        cost_estimate=pl.CostEstimate(
            flops=8 * size * size * frames, bytes_accessed=20 * size * frames, transcendentals=0),
    )(left, right, moved)


def per_device(activity, plan):
    scores = standardize(activity)
    size, frames = scores.shape
    parts = scores.reshape(PARTS, size // PARTS, frames)
    blocks = lax.axis_size("blk")
    first_last = plan[0] == blocks - 1
    distance = jnp.where(first_last, plan[1], plan[0])
    highs = [partial(gather, high=h) for h in range(blocks // ROW)]
    lows = [partial(products, low=k) for k in range(ROW)]
    gathered = lax.switch(distance // ROW, highs, parts, scores)
    both = lax.switch(distance % ROW, lows, *gathered)
    return jnp.where(first_last, both, both[::-1])


def solution(mesh):
    in_specs = (P("blk", "frm"), P())
    out_specs = P(None, ("blk", "frm"), None)
    return jax.shard_map(
        per_device, mesh=mesh, in_specs=in_specs, out_specs=out_specs, check_vma=False
    )
```

```python
from functools import partial
import math

import jax
import jax.numpy as jnp
from jax import lax
from jax.experimental import pallas as pl
from jax.experimental.pallas import tpu as pltpu
from jax.sharding import PartitionSpec as P

EPS = 1e-05
MESH = pl.DeviceIdType.MESH
PARTS = 4
CHUNKS = 7
TILE = 256
ROW = 8
DEPTH = 512
AHEAD = 4
FLIGHT = 2


def standardize(activity):
    mean = jnp.mean(activity, axis=1, keepdims=True)
    centred = activity - mean
    spread = jnp.mean(centred * centred, axis=1, keepdims=True)
    return (centred * lax.rsqrt(spread + EPS)).astype(jnp.bfloat16)


def loop(stop, act, start=0):
    def body(i, carry):
        act(i)
        return carry
    lax.fori_loop(start, stop, body, 0)


def remote(src, dst, send, recv, device):
    return pltpu.make_async_remote_copy(
        src_ref=src, dst_ref=dst, send_sem=send, recv_sem=recv, device_id=device, device_id_type=MESH)


class Place:
    def __init__(self):
        self.blocks = lax.axis_size("blk")
        self.b, self.f = lax.axis_index("blk"), lax.axis_index("frm")
        self.half = self.f // 2
        self.inner = self.f * (3 - self.f) // 2
        self.outer = 1 - self.inner
        self.centre, self.end, self.other = 1 + self.half, 3 * self.half, 2 - self.half

    def crossing(self, one, two):
        return lax.rem(one // ROW + two // ROW, 2)

    def target(self, shift):
        block = lax.rem(self.b + (self.blocks - shift), self.blocks)
        return block, 1 + lax.rem(self.half + self.crossing(self.b, block), 2)

    def source(self, shift):
        block = lax.rem(self.b + shift, self.blocks)
        return block, lax.rem(self.half + self.crossing(self.b, block), 2)

    def far(self, i):
        return (1 - self.half) * (3 - i) + self.half * i

    def near(self, i):
        return self.half * (3 - i) + (1 - self.half) * i


def greet(block, frm):
    pl.semaphore_signal(pltpu.get_barrier_semaphore(), inc=1, device_id=(block, frm), device_id_type=MESH)


def gather_kernel(high, parts_ref, scores_ref, left, right, moved,
                  own_sem, h_send, h_recv, pp_send, pp_recv, fwd_send, fwd_recv, move_send, move_recv):
    size, frames = scores_ref.shape
    piece = size // CHUNKS
    at = Place()
    mirrored = high % 2
    shift = at.blocks - 1

    def lanes(frame_slice):
        slot = 3 - frame_slice if mirrored else frame_slice
        return pl.ds(pl.multiple_of(slot * frames, 128), frames)

    def part_in(i):
        return remote(parts_ref.at[at.near(i)], left.at[i, :, lanes(at.f)], h_send.at[0, i], h_recv.at[0, i],
                      (at.b, at.centre))

    def part_across(i):
        return remote(parts_ref.at[at.far(i)], left.at[i, :, lanes(at.f)], h_send.at[1, i],
                      h_recv.at[1 + at.outer, i], (at.b, at.other))

    def part_arrives(i, kind):
        return remote(parts_ref.at[i], left.at[i, :, lanes(at.f)], h_send.at[0, i], h_recv.at[kind, i],
                      (at.b, at.other))

    def part_own(i):
        return pltpu.make_async_copy(parts_ref.at[at.near(i)], left.at[i, :, lanes(at.f)], own_sem.at[i])

    def rows_of(q):
        return pl.ds(pl.multiple_of(q * piece, 16), piece)

    aim = at.target(shift)
    _, side = at.source(shift)

    def slice_out(q):
        rows = rows_of(q)
        return remote(scores_ref.at[rows], right.at[rows, lanes(at.f)], pp_send.at[q], pp_recv.at[q, at.outer], aim)

    def slice_arrives(q, kind):
        rows = rows_of(q)
        return remote(scores_ref.at[rows], right.at[rows, lanes(at.f)], pp_send.at[q], pp_recv.at[q, kind],
                      (at.b, at.other))

    def pass_on(q, kind):
        where = right.at[rows_of(q), lanes((1 + side) * (1 - kind) + 3 * side * kind)]
        return remote(where, where, fwd_send.at[q, kind], fwd_recv.at[q, kind], (at.b, at.other))

    place = 3 - at.f if mirrored else at.f
    if high:
        move = remote(scores_ref, moved, move_send.at[0], move_recv.at[0],
                      (lax.rem(at.b + (at.blocks - ROW * high), at.blocks), place))
        greet(lax.rem(at.b + ROW * high, at.blocks), place)
    else:
        move = pltpu.make_async_copy(scores_ref, moved, move_send.at[0])

    @pl.when(at.inner == 0)
    def _():
        greet(at.b, at.centre)

    @pl.when(at.inner == 1)
    def _():
        loop(2, lambda i: part_own(i).start())
        greet(at.b, at.end)
        greet(at.b, 3 - at.end)
        greet(at.b, at.other)
        block, side = at.source(shift)
        greet(block, 1 + side)
        greet(block, 3 * side)

    pl.semaphore_wait(pltpu.get_barrier_semaphore(), 3 + (1 if high else 0))

    loop(2, lambda i: part_across(i).start())
    loop(FLIGHT, lambda q: slice_out(q).start())
    if not mirrored:
        move.start()

    def next_slice(q):
        slice_out(q).wait_send()

        @pl.when(q + FLIGHT < CHUNKS)
        def _():
            slice_out(q + FLIGHT).start()

    @pl.when(at.inner == 0)
    def _():
        if mirrored:
            move.start()
        loop(CHUNKS, next_slice)
        loop(2, lambda i: part_in(i).start())
        loop(2, lambda i: part_in(i).wait_send())

    @pl.when(at.inner == 1)
    def _():
        def forward(q):
            next_slice(q)

            def one(kind):
                slice_arrives(q, kind).wait_recv()
                pass_on(q, kind).start()
            loop(2, one)
            if mirrored:
                @pl.when(q == CHUNKS // 2)
                def _():
                    move.start()
        loop(CHUNKS, forward)

        def rows_there(i):
            part_own(i).wait()
            loop(3, lambda kind: part_arrives(i, kind).wait_recv())
        loop(2, rows_there)
        loop(CHUNKS, lambda q: loop(2, lambda kind: pass_on(q, kind).wait_recv()))
        loop(CHUNKS, lambda q: loop(2, lambda kind: pass_on(q, kind).wait_send()))

    loop(2, lambda i: part_across(i).wait_send())
    move.wait()


def product_kernel(low, factor, left_ref, right_ref, moved, out_ref, left, right, fin, acc,
                   own_sem, pp_send, pp_recv, fwd_send, fwd_recv, out_send, out_recv, keep_sem):
    size, frames = moved.shape
    piece = size // CHUNKS
    tiles = -(-size // TILE)
    at = Place()

    def lanes(slot):
        return pl.ds(pl.multiple_of(slot * frames, 128), frames)

    def rows_of(q):
        return pl.ds(pl.multiple_of(q * piece, 16), piece)

    block, centre = at.target(low)
    aim = (block, centre * at.inner + 3 * (centre - 1) * at.outer) if low else (at.b, at.centre)
    origin, side = at.source(low)

    def slice_out(q):
        rows = rows_of(q)
        return remote(moved.at[rows], right.at[1, rows, lanes(at.f)], pp_send.at[q], pp_recv.at[q, at.outer], aim)

    def slice_arrives(q, kind):
        rows = rows_of(q)
        return remote(moved.at[rows], right.at[1, rows, lanes(at.f)], pp_send.at[q], pp_recv.at[q, kind],
                      (at.b, at.other))

    def next_slice(q):
        slice_out(q).wait_send()

        @pl.when(q + FLIGHT < CHUNKS)
        def _():
            slice_out(q + FLIGHT).start()

    def hand_over(q):
        where = right.at[1, rows_of(q), lanes(3 * side)]
        return remote(where, where, fwd_send.at[q, 1], pp_recv.at[q, 1], (at.b, at.centre))

    def slice_own(q):
        rows = rows_of(q)
        return pltpu.make_async_copy(moved.at[rows], right.at[1, rows, lanes(at.f)], pp_send.at[q])

    def pass_on(q, kind):
        where = right.at[1, rows_of(q), lanes((1 + side) * (1 - kind) + 3 * side * kind)]
        return remote(where, where, fwd_send.at[q, kind], fwd_recv.at[q, kind], (at.b, at.other))

    def tile(j, act):
        @pl.when(j < tiles - 1)
        def _():
            act(pl.ds(pl.multiple_of(j * TILE, TILE), TILE))

        @pl.when(j == tiles - 1)
        def _():
            act(pl.ds((tiles - 1) * TILE, size - (tiles - 1) * TILE))

    def result_out(r, j, cols):
        return remote(fin.at[r, 0, :, cols], out_ref.at[r, :, cols], out_send.at[r, j], out_recv.at[r, j],
                      (at.b, at.end))

    def result_kept(r, j, cols):
        return pltpu.make_async_copy(fin.at[r, 1, :, cols], out_ref.at[r, :, cols], keep_sem.at[r, j])

    def work(r, j):
        def columns(cols):
            def half_rows(i):
                def add(k):
                    deep = pl.ds(pl.multiple_of(k * DEPTH, 128), DEPTH)
                    acc[:, :cols.size] += lax.dot_general(
                        left[i, :, deep], right[r, cols, deep], (((1,), (1,)), ((), ())),
                        preferred_element_type=jnp.float32)
                acc[...] = jnp.zeros_like(acc)
                loop(PARTS * frames // DEPTH, add)
                fin[r, i, :, cols] = (acc[:, :cols.size] * factor).astype(fin.dtype)
            loop(2, half_rows)
            result_out(r, j, cols).start()
            result_kept(r, j, cols).start()
        tile(j, columns)

    loads = [
        pltpu.make_async_copy(left_ref, left, own_sem.at[0]),
        pltpu.make_async_copy(right_ref, right.at[0], own_sem.at[1]),
    ]
    barrier = pltpu.get_barrier_semaphore()

    @pl.when(at.inner == 0)
    def _():
        greet(at.b, at.centre)
        if low:
            greet(origin, 3 * side)
        pl.semaphore_wait(barrier, 2 if low else 1)
        loop(FLIGHT, lambda q: slice_out(q).start())
        if low:
            def relay(q):
                next_slice(q)
                slice_arrives(q, 1).wait_recv()
                hand_over(q).start()
            loop(CHUNKS, relay)
            loop(CHUNKS, lambda q: hand_over(q).wait_send())
        else:
            loop(CHUNKS, next_slice)
        for r in range(2):
            loop(tiles, lambda j: tile(j, lambda cols: result_out(r, j, cols).wait_recv()))

    @pl.when(at.inner == 1)
    def _():
        greet(at.b, at.other)
        greet(at.b, at.end)
        if low:
            greet(origin, 1 + side)
            pl.semaphore_wait(barrier, 3)
            loop(FLIGHT, lambda q: slice_out(q).start())
        else:
            loop(CHUNKS, lambda q: slice_own(q).start())
            pl.semaphore_wait(barrier, 2)
        for load in loads:
            load.start()

        def forward(q):
            if low:
                next_slice(q)
                slice_arrives(q, 0).wait_recv()
            else:
                slice_own(q).wait()
            pass_on(q, 0).start()
            slice_arrives(q, 1).wait_recv()
            pass_on(q, 1).start()
        for load in loads:
            load.wait()

        def first_round(j):
            work(0, j)

            @pl.when(j >= tiles - AHEAD)
            def _():
                forward(j - (tiles - AHEAD))
        loop(tiles, first_round)

        def step(t):
            @pl.when(t + AHEAD < CHUNKS)
            def _():
                forward(t + AHEAD)
            loop(2, lambda kind: pass_on(t, kind).wait_recv())
            loop(jnp.where(t == CHUNKS - 1, tiles, (t + 1) * piece // TILE), lambda j: work(1, j), t * piece // TILE)
        loop(CHUNKS, step)

        def drain(q):
            loop(2, lambda kind: pass_on(q, kind).wait_send())
        loop(CHUNKS, drain)

        def drain_results(t):
            r, j = t // tiles, lax.rem(t, tiles)

            def act(cols):
                result_out(r, j, cols).wait_send()
                result_kept(r, j, cols).wait()
            tile(j, act)
        loop(2 * tiles, drain_results)


ANY = pl.BlockSpec(memory_space=pl.ANY)


def gather(parts, scores, high):
    size, frames = scores.shape
    rows = size // PARTS
    dma = pltpu.SemaphoreType.DMA
    return pl.pallas_call(
        partial(gather_kernel, high),
        name="gather_rows",
        out_shape=[
            jax.ShapeDtypeStruct((2, rows, PARTS * frames), jnp.bfloat16),
            jax.ShapeDtypeStruct((size, PARTS * frames), jnp.bfloat16),
            jax.ShapeDtypeStruct((size, frames), jnp.bfloat16),
        ],
        in_specs=[ANY] * 2,
        out_specs=[ANY] * 3,
        scratch_shapes=[
            dma((2,)), dma((2, 2)), dma((3, 2)), dma((CHUNKS,)), dma((CHUNKS, 2)), dma((CHUNKS, 2)), dma((CHUNKS, 2)),
            dma((1,)), dma((1,)),
        ],
        compiler_params=pltpu.CompilerParams(
            collective_id=high, has_side_effects=True, vmem_limit_bytes=4 * 2**20),
        cost_estimate=pl.CostEstimate(flops=0, bytes_accessed=20 * size * frames, transcendentals=0),
    )(parts, scores)


def products(left, right, moved, low):
    size, frames = moved.shape
    rows = size // PARTS
    tiles = -(-size // TILE)
    factor = 1.0 / math.sqrt(frames * PARTS)
    dma = pltpu.SemaphoreType.DMA
    return pl.pallas_call(
        partial(product_kernel, low, factor),
        name="pair_products",
        out_shape=jax.ShapeDtypeStruct((2, rows, size), jnp.bfloat16),
        in_specs=[ANY] * 3,
        out_specs=ANY,
        scratch_shapes=[
            pltpu.VMEM((2, rows, PARTS * frames), jnp.bfloat16),
            pltpu.VMEM((2, size, PARTS * frames), jnp.bfloat16),
            pltpu.VMEM((2, 2, rows, size), jnp.bfloat16),
            pltpu.VMEM((rows, TILE), jnp.float32),
            dma((2,)), dma((CHUNKS,)), dma((CHUNKS, 2)), dma((CHUNKS, 2)), dma((CHUNKS, 2)),
            dma((2, tiles)), dma((2, tiles)), dma((2, tiles)),
        ],
        compiler_params=pltpu.CompilerParams(
            collective_id=ROW + low, has_side_effects=True, vmem_limit_bytes=32 * 2**20),
        cost_estimate=pl.CostEstimate(
            flops=8 * size * size * frames, bytes_accessed=20 * size * frames, transcendentals=0),
    )(left, right, moved)


def per_device(activity, plan):
    scores = standardize(activity)
    size, frames = scores.shape
    parts = scores.reshape(PARTS, size // PARTS, frames)
    blocks = lax.axis_size("blk")
    first_last = plan[0] == blocks - 1
    distance = jnp.where(first_last, plan[1], plan[0])
    highs = [partial(gather, high=h) for h in range(blocks // ROW)]
    lows = [partial(products, low=k) for k in range(ROW)]
    gathered = lax.switch(distance // ROW, highs, parts, scores)
    both = lax.switch(distance % ROW, lows, *gathered)
    return jnp.where(first_last, both, both[::-1])


def solution(mesh):
    in_specs = (P("blk", "frm"), P())
    out_specs = P(None, ("blk", "frm"), None)
    return jax.shard_map(
        per_device, mesh=mesh, in_specs=in_specs, out_specs=out_specs, check_vma=False
    )
```
